32 devices in a mesh: ctx: 4 (over x, core), exp: 8 (over z, y).
Axes of the slice: x: 2, y: 2, z: 4, core: 2. Of those that a mesh axis runs over, the one named last changes fastest.
Arguments:
- hidden_in: bfloat16 [8, 512, 2048], P('exp', 'ctx'), may hold values from -6 to 6
- grad_out: bfloat16 [8, 512, 2048], P('exp', 'ctx'), may hold values from -6 to 6
- post_gain: float32 [2048], replicated, may hold values from 0.1 to 1.9
- route_ids: int32 [8, 512, 10], P('exp', 'ctx'), may hold values from 0 to 511, as said below
- route_weight: float32 [8, 512, 10], P('exp', 'ctx'), may hold values from 0.02 to 0.3
- gate_up: bfloat16 [32, 2048, 1024], P(('ctx', 'exp')), may hold values from -0.125 to 0.125
- down_proj: bfloat16 [32, 512, 2048], P(('ctx', 'exp')), may hold values from -0.25 to 0.25
- query_in: bfloat16 [8, 512, 1024], P('exp', 'ctx'), may hold values from -6 to 6
- key_in: bfloat16 [8, 512, 1024], P('exp', 'ctx'), may hold values from -6 to 6
- value_in: bfloat16 [8, 512, 2048], P('exp', 'ctx'), may hold values from -6 to 6
- gate_in: bfloat16 [8, 512, 2048], P('exp', 'ctx'), may hold values from -6 to 6
- decay_logit: bfloat16 [8, 512, 16], P('exp', 'ctx'), may hold values from -12 to 0.5
- beta_logit: bfloat16 [8, 512, 16], P('exp', 'ctx'), may hold values from -6 to 6
- head_gain: float32 [128], replicated, may hold values from 0.1 to 1.9
- out_proj: bfloat16 [2048, 2048], P(None, 'ctx'), may hold values from -0.125 to 0.125
Outputs:
- grad_hidden: bfloat16 [8, 512, 2048], P('exp', 'ctx')
- grad_query: bfloat16 [8, 512, 1024], P('exp', 'ctx')
- grad_key: bfloat16 [8, 512, 1024], P('exp', 'ctx')
- grad_value: bfloat16 [8, 512, 2048], P('exp', 'ctx')
- grad_gate: bfloat16 [8, 512, 2048], P('exp', 'ctx')
- grad_decay: bfloat16 [8, 512, 16], P('exp', 'ctx')
- grad_beta: bfloat16 [8, 512, 16], P('exp', 'ctx')
- grad_gate_up: bfloat16 [32, 2048, 1024], P(('ctx', 'exp'))
- grad_down: bfloat16 [32, 512, 2048], P(('ctx', 'exp'))
- grad_out_proj: float32 [2048, 2048], P('exp', 'ctx')
The draws below stay inside these ranges and needn't reach their ends.
Inputs may be any that keep to these rules, and one draw needn't show every extreme that they name: `route_ids`: each token names 10 different experts. The 128 positions of a sequence on one device name no expert more than 4 times, and one expert below 32, the same on every device, is named exactly 4 times by them.
All inputs are finite; a program needn't handle non-finite values.
Results may differ from the reference program's by a relative error of at most 0.014.
Values may be sent and summed in bfloat16 or wider, within the bound.
A program may use at most 128 MiB of HBM per device.

```python
import jax
import jax.numpy as jnp
from jax import lax

D = 2048
F = 512
EXPERTS = 512
EXPERTS_PER_TOKEN = 10
VH = 16
DK = 128
BLOCK = 128
DEVICE_TOKENS = 128
EXPERT_ROW_LIMIT = 4
HELD = 32
SEQUENCE_COUNT = 8
WINDOW_LENGTH = 512
TOKENS = 4096
KD = 1024
VD = 2048


def draw_route_ids(key, part):
    block_total = SEQUENCE_COUNT * WINDOW_LENGTH // DEVICE_TOKENS
    hottest = jax.random.randint(jax.random.fold_in(key, 7), (), 0, HELD)

    def one_block(index):
        block_key = jax.random.fold_in(key, index)
        first, second, third_piece, fourth_piece = jax.random.split(block_key, 4)
        ordering = (hottest + 1 + jax.random.permutation(first, EXPERTS - 1)) % EXPERTS
        offset = jax.random.randint(second, (), 0, EXPERTS - 1)
        token_rows = jnp.arange(DEVICE_TOKENS)
        places = (offset + token_rows[:, None] * EXPERTS_PER_TOKEN + jnp.arange(EXPERTS_PER_TOKEN)[None, :]) % (EXPERTS - 1)
        chosen = ordering[places]
        holder_rows = jax.random.permutation(third_piece, DEVICE_TOKENS) < EXPERT_ROW_LIMIT
        chosen_slot_index = jax.random.randint(fourth_piece, (DEVICE_TOKENS,), 0, EXPERTS_PER_TOKEN)
        slot_assigned = holder_rows[:, None] & (jnp.arange(EXPERTS_PER_TOKEN)[None, :] == chosen_slot_index[:, None])
        return jnp.where(slot_assigned, hottest, chosen)
    every_block = jax.vmap(one_block)(jnp.arange(block_total))
    return every_block.reshape(SEQUENCE_COUNT, WINDOW_LENGTH, EXPERTS_PER_TOKEN).astype(jnp.int32)


def draw_decay_logit(key, part):
    first, second, third_piece, fourth_piece, fifth = jax.random.split(key, 5)
    quick = jax.random.uniform(first, (VH,)) < 0.5
    spread = jnp.exp(jax.random.uniform(second, (SEQUENCE_COUNT, 1, VH), minval=0.0, maxval=0.7))
    rough = jnp.exp(jax.random.uniform(third_piece, (SEQUENCE_COUNT, WINDOW_LENGTH, VH), minval=-0.7, maxval=0.7))
    base_rate = jnp.where(quick, 1.0 / 40.0, 0.3 / WINDOW_LENGTH)
    rates = base_rate * spread * rough
    spill_position = jax.random.randint(fourth_piece, (SEQUENCE_COUNT, 2), 0, WINDOW_LENGTH)
    spilling_over = jnp.any(jnp.arange(WINDOW_LENGTH)[None, :, None] == spill_position[:, None, :], axis=-1)
    losses = jax.random.uniform(fifth, (SEQUENCE_COUNT, WINDOW_LENGTH, VH), minval=0.2, maxval=0.5)
    rates = jnp.where(spilling_over[:, :, None], -jnp.log1p(-losses), rates)
    return jnp.log(jnp.expm1(rates)).astype(jnp.float32).astype(jnp.bfloat16)


def coherent_mask(key):
    picked = jax.random.randint(jax.random.fold_in(key, 70001), (SEQUENCE_COUNT,), 0, WINDOW_LENGTH // BLOCK)
    block_of = jnp.arange(WINDOW_LENGTH) // BLOCK
    return block_of[None, :] == picked[:, None]


def draw_key_in(key, part):
    first, second = jax.random.split(jax.random.fold_in(key, 70003))
    coherent = coherent_mask(key)[:, :, None]
    shape = (SEQUENCE_COUNT, WINDOW_LENGTH, KD)
    direction = jnp.where(jax.random.bernoulli(second, 0.5, (SEQUENCE_COUNT, 1, KD)), 1.0, -1.0)
    noise = jax.random.normal(first, shape)
    values = jnp.where(coherent, 4.0 * direction + noise, noise)
    return jnp.clip(values, -6.0, 6.0).astype(jnp.float32).astype(jnp.bfloat16)


def draw_beta_logit(key, part):
    first, second = jax.random.split(jax.random.fold_in(key, 70005))
    coherent = coherent_mask(key)[:, :, None]
    shape = (SEQUENCE_COUNT, WINDOW_LENGTH, VH)
    spread = 1.5 * jax.random.normal(first, shape)
    strong = 4.0 + 0.5 * jax.random.normal(second, shape)
    values = jnp.where(coherent, strong, spread)
    return jnp.clip(values, -6.0, 6.0).astype(jnp.float32).astype(jnp.bfloat16)


def steps_of(own_key, shape, shards, smallest, high):
    loudness, own = 1.0, jax.random.fold_in(own_key, 6)
    for dim, shards_of in shards:
        heights = jnp.exp(jax.random.uniform(jax.random.fold_in(own, dim), (shards_of,), jnp.float32, smallest / len(shards), high / len(shards)))
        loudness = loudness * jnp.repeat(heights, shape[dim] // shards_of).reshape([-1 if axis == dim else 1 for axis in range(len(shape))])
    return loudness


def scatter_about(rng, extent, scale, bound, cuts=(), kind=jnp.bfloat16):
    values = scale * jax.random.normal(rng, extent, jnp.float32)
    if cuts:
        values = values * steps_of(rng, extent, cuts, -0.22, 0.18)
    return jnp.clip(values, -bound, bound).astype(kind)


def setup_inputs(seed: int = 0) -> dict:
    key_of = jax.random.split(jax.random.key(seed), 16)
    return {
        "hidden_in": scatter_about(key_of[0], (SEQUENCE_COUNT, WINDOW_LENGTH, D), 1.0, 6.0, ((0, 8), (1, 4))),
        "grad_out": scatter_about(key_of[1], (SEQUENCE_COUNT, WINDOW_LENGTH, D), 1.0, 6.0, ((0, 8), (1, 4))),
        "post_gain": jnp.clip(1.0 + 0.18 * jax.random.normal(key_of[2], (D,), jnp.float32), 0.1, 1.9),
        "route_ids": draw_route_ids(jax.random.fold_in(key_of[15], 71), 0),
        "route_weight": jnp.clip(0.02 + 0.28 * jax.random.uniform(key_of[4], (SEQUENCE_COUNT, WINDOW_LENGTH, EXPERTS_PER_TOKEN), jnp.float32) ** steps_of(key_of[4], (SEQUENCE_COUNT, WINDOW_LENGTH, EXPERTS_PER_TOKEN), ((0, 8), (1, 4)), -0.2, 0.2), 0.02, 0.3),
        "gate_up": scatter_about(key_of[5], (HELD, D, 2 * F), D ** -0.5, 0.125, ((0, 32),)),
        "down_proj": scatter_about(key_of[6], (HELD, F, D), F ** -0.5, 0.25, ((0, 32),)),
        "query_in": scatter_about(key_of[7], (SEQUENCE_COUNT, WINDOW_LENGTH, KD), 1.0, 6.0, ((0, 8), (1, 4))),
        "key_in": draw_key_in(jax.random.fold_in(key_of[15], 71), 0),
        "value_in": scatter_about(key_of[9], (SEQUENCE_COUNT, WINDOW_LENGTH, VD), 1.0, 6.0, ((0, 8), (1, 4))),
        "gate_in": scatter_about(key_of[10], (SEQUENCE_COUNT, WINDOW_LENGTH, VD), 1.0, 6.0, ((0, 8), (1, 4))),
        "decay_logit": draw_decay_logit(jax.random.fold_in(key_of[15], 71), 0),
        "beta_logit": draw_beta_logit(jax.random.fold_in(key_of[15], 71), 0),
        "head_gain": jnp.clip(1.0 + 0.18 * jax.random.normal(key_of[13], (DK,), jnp.float32), 0.1, 1.9),
        "out_proj": scatter_about(key_of[14], (D, VD), VD ** -0.5, 0.125, ((1, 4),)),
    }


precise = lax.Precision.HIGHEST

def post_norm(hidden, gains):
    inverse_rms = lax.rsqrt(lax.optimization_barrier(jnp.mean(hidden * hidden, axis=-1, keepdims=True)) + 1e-06)
    return hidden * inverse_rms * gains

def block_step(memory, pieces):
    queries, key_rows, value_rows, strength, log_decay = pieces
    block_len = queries.shape[1]
    positions = jnp.arange(block_len)
    within = positions[:, None] >= positions[None, :]
    strict = positions[:, None] > positions[None, :]
    cumulative = jnp.cumsum(log_decay, axis=1)
    decay_mat = jnp.where(within, jnp.exp(jnp.where(within, cumulative[:, :, None] - cumulative[:, None, :], 0.0)), 0.0)
    inner_keys = jnp.einsum('htd,hsd->hts', key_rows, key_rows, precision=precise)
    lower_part = jnp.where(strict, strength[:, :, None] * decay_mat * inner_keys, 0.0)
    system = lower_part + jnp.eye(block_len, dtype=lower_part.dtype)
    recalled = jnp.einsum('hvd,htd->htv', memory, key_rows, precision=precise)
    rising = jnp.exp(cumulative)
    target = strength[:, :, None] * (value_rows - rising[:, :, None] * recalled)
    update = lax.linalg.triangular_solve(system, target, left_side=True, lower=True, unit_diagonal=True)
    scores = jnp.einsum('htd,hsd->hts', queries, key_rows, precision=precise) * decay_mat
    output = rising[:, :, None] * jnp.einsum('hvd,htd->htv', memory, queries, precision=precise)
    output = output + jnp.einsum('hts,hsv->htv', scores, update, precision=precise)
    last_log = cumulative[:, -1]
    fading = jnp.exp(last_log[:, None] - cumulative)
    memory = jnp.exp(last_log)[:, None, None] * memory + jnp.einsum('hsv,hsd->hvd', update * fading[:, :, None], key_rows, precision=precise)
    return (memory, output)

def gated_delta(query_rows, key_rows, value_rows, gate_rows, decay_rows, beta_rows, head_gain):
    length = query_rows.shape[0]
    head_dim = head_gain.shape[0]
    key_heads = query_rows.shape[1] // head_dim
    value_heads = value_rows.shape[1] // head_dim
    group_size = value_heads // key_heads

    def unit_rows(tensor):
        shaped = tensor.reshape(length, key_heads, head_dim)
        shaped = shaped * lax.rsqrt(lax.optimization_barrier(jnp.sum(shaped * shaped, axis=-1, keepdims=True)) + 1e-06)
        return jnp.repeat(shaped, group_size, axis=1)
    queries_unit = unit_rows(query_rows) * head_dim ** (-0.5)
    keys_unit = unit_rows(key_rows)
    values_all = value_rows.reshape(length, value_heads, head_dim)
    strength = jax.nn.sigmoid(beta_rows)
    log_decay = -jax.nn.softplus(decay_rows)
    block_count = length // BLOCK

    def to_blocks(tensor):
        moved_axes = jnp.moveaxis(tensor, 0, 1)
        shaped = moved_axes.reshape((value_heads, block_count, BLOCK) + tensor.shape[2:])
        return jnp.moveaxis(shaped, 1, 0)
    initial = jnp.zeros((value_heads, head_dim, head_dim), query_rows.dtype)
    final_memory, outputs = lax.scan(block_step, initial, (to_blocks(queries_unit), to_blocks(keys_unit), to_blocks(values_all), to_blocks(strength), to_blocks(log_decay)))
    output = jnp.moveaxis(outputs, 0, 1).reshape(value_heads, length, head_dim)
    output = jnp.moveaxis(output, 0, 1)
    gates_all = gate_rows.reshape(length, value_heads, head_dim)
    normed = output * lax.rsqrt(lax.optimization_barrier(jnp.mean(output * output, axis=-1, keepdims=True)) + 1e-06) * head_gain
    return (normed * jax.nn.silu(gates_all)).reshape(length, value_heads * head_dim)

def expert_backward(rows_in, rows_grad, gate_up, down_proj):
    hidden_units = down_proj.shape[0]
    contract_rows = (((1,), (1,)), ((), ()))
    contract_cols = (((0,), (0,)), ((), ()))
    projected = jnp.dot(rows_in.astype(jnp.float32), gate_up.astype(jnp.float32), preferred_element_type=jnp.float32)
    gate_part = projected[:, :hidden_units]
    up_part = projected[:, hidden_units:]
    sigma = jax.nn.sigmoid(gate_part)
    activated = gate_part * sigma
    product = (activated * up_part).astype(jnp.bfloat16)
    grad_act = lax.dot_general(rows_grad.astype(jnp.float32), down_proj.astype(jnp.float32), contract_rows, preferred_element_type=jnp.float32)
    grad_gate_part = grad_act * up_part * sigma * (1.0 + gate_part * (1.0 - sigma))
    grad_up_part = grad_act * activated
    grad_projected = jnp.concatenate([grad_gate_part, grad_up_part], axis=1).astype(jnp.bfloat16)
    rows_back = lax.dot_general(grad_projected.astype(jnp.float32), gate_up.astype(jnp.float32), contract_rows, preferred_element_type=jnp.float32).astype(jnp.bfloat16)
    weight_gate_up = lax.dot_general(rows_in.astype(jnp.float32), grad_projected.astype(jnp.float32), contract_cols, preferred_element_type=jnp.float32).astype(jnp.bfloat16)
    weight_down = lax.dot_general(product.astype(jnp.float32), rows_grad.astype(jnp.float32), contract_cols, preferred_element_type=jnp.float32).astype(jnp.bfloat16)
    return (rows_back, weight_gate_up, weight_down)

def reference(hidden_in, grad_out, post_gain, route_ids, route_weight, gate_up, down_proj, query_in, key_in, value_in, gate_in, decay_logit, beta_logit, head_gain, out_proj):
    flat_hidden = hidden_in.reshape(TOKENS, D).astype(jnp.float32)
    normed, norm_back = jax.vjp(lambda tensor: post_norm(tensor, post_gain), flat_hidden)
    moe_input = normed.astype(jnp.bfloat16)
    flat_grad = grad_out.reshape(TOKENS, D)
    slot_ids = route_ids.reshape(-1)
    slot_weights = route_weight.reshape(-1)
    input_ext = jnp.concatenate([moe_input, jnp.zeros((1, D), jnp.bfloat16)], axis=0)
    grad_ext = jnp.concatenate([flat_grad, jnp.zeros((1, D), jnp.bfloat16)], axis=0)
    weight_ext = jnp.concatenate([slot_weights, jnp.zeros((1,), jnp.float32)], axis=0)
    rows_most = HELD * EXPERT_ROW_LIMIT

    def per_expert(totals, expert):
        slots, = jnp.nonzero(slot_ids == expert, size=rows_most, fill_value=TOKENS * EXPERTS_PER_TOKEN)
        tokens_of = slots // EXPERTS_PER_TOKEN
        rows_in = input_ext[tokens_of]
        rows_grad = (grad_ext[tokens_of].astype(jnp.float32) * weight_ext[slots][:, None]).astype(jnp.bfloat16)
        rows_back, weight_gate_up, weight_down = expert_backward(rows_in, rows_grad, gate_up[expert], down_proj[expert])
        totals = totals.at[tokens_of].add(rows_back.astype(jnp.float32), mode='drop')
        return (totals, (weight_gate_up, weight_down))
    moe_grad, (grad_gate_up, grad_down) = lax.scan(per_expert, jnp.zeros((TOKENS, D), jnp.float32), jnp.arange(HELD, dtype=jnp.int32))
    norm_grad, = norm_back(moe_grad)
    grad_hidden = (flat_grad.astype(jnp.float32) + norm_grad).astype(jnp.bfloat16).reshape(SEQUENCE_COUNT, WINDOW_LENGTH, D)
    scale_factor = float(TOKENS) ** (-0.5)

    def per_sequence(totals, index):

        def forward(query_rows, key_rows, value_rows, gate_rows, decay_rows, beta_rows):
            return gated_delta(query_rows, key_rows, value_rows, gate_rows, decay_rows, beta_rows, head_gain)
        gated, core_back = jax.vjp(forward, query_in[index].astype(jnp.float32), key_in[index].astype(jnp.float32), value_in[index].astype(jnp.float32), gate_in[index].astype(jnp.float32), decay_logit[index].astype(jnp.float32), beta_logit[index].astype(jnp.float32))
        sequence_grad = grad_hidden[index]
        grad_gated = jnp.dot(sequence_grad.astype(jnp.float32), out_proj.astype(jnp.float32), preferred_element_type=jnp.float32)
        gradients = core_back(grad_gated)
        term = lax.dot_general(sequence_grad.astype(jnp.float32), gated.astype(jnp.bfloat16).astype(jnp.float32), (((0,), (0,)), ((), ())), preferred_element_type=jnp.float32)
        totals = totals + scale_factor * term
        return (totals, tuple((piece.astype(jnp.bfloat16) for piece in gradients)))
    grad_out_proj, gradients = lax.scan(per_sequence, jnp.zeros((D, VD), jnp.float32), jnp.arange(SEQUENCE_COUNT, dtype=jnp.int32))
    return (grad_hidden, gradients[0], gradients[1], gradients[2], gradients[3], gradients[4], gradients[5], grad_gate_up, grad_down, grad_out_proj)
```

```python
import functools

import jax
import jax.numpy as jnp
from jax import lax
from jax.experimental import pallas as pl
from jax.experimental.pallas import tpu as pltpu
from jax.sharding import PartitionSpec as P

BLOCK = 128
LANES = 128
f32 = jnp.float32
bf16 = jnp.bfloat16


def split(tensor):
    high = tensor.astype(bf16)
    return high, (tensor - high.astype(f32)).astype(bf16)


def full(left, right):
    return [(left[0], right[0]), (left[1], right[0]), (left[0], right[1])]


def left_exact(left, right):
    return [(left, right[0]), (left, right[1])]


def right_exact(left, right):
    return [(left[0], right), (left[1], right)]


def contract(pairs, left_dim, right_dim):
    left = jnp.concatenate([pair[0] for pair in pairs], axis=left_dim)
    right = jnp.concatenate([pair[1] for pair in pairs], axis=right_dim)
    return lax.dot_general(
        left, right, (((left_dim,), (right_dim,)), ((), ())), preferred_element_type=f32
    )


def sigmoid(tensor):
    return 1.0 / (1.0 + jnp.exp(-tensor))


def row_sum(tensor):
    return jnp.sum(tensor, axis=1, keepdims=True)


def offsets(key_heads, value_heads):
    query_at = 0
    key_at = key_heads * LANES
    value_at = 2 * key_heads * LANES
    gate_at = value_at + value_heads * LANES
    small_at = gate_at + value_heads * LANES
    return query_at, key_at, value_at, gate_at, small_at


def shared(x_ref, key_heads, value_heads):
    query_at, key_at, _, _, small_at = offsets(key_heads, value_heads)
    row = lax.broadcasted_iota(jnp.int32, (BLOCK, BLOCK), 0)
    col = lax.broadcasted_iota(jnp.int32, (BLOCK, BLOCK), 1)
    within = row >= col
    small = x_ref[:, small_at : small_at + LANES].astype(f32)
    log_decay = -(jnp.maximum(small, 0.0) + jnp.log1p(jnp.exp(-jnp.abs(small))))
    log_decay = jnp.where(col < value_heads, log_decay, 0.0)
    cumulative = jnp.dot(
        within.astype(f32),
        log_decay,
        precision=lax.Precision.HIGHEST,
        preferred_element_type=f32,
    )
    strengths = sigmoid(small)
    keys, queries = [], []
    packed = cumulative
    for j in range(key_heads):
        q = x_ref[:, query_at + j * LANES : query_at + (j + 1) * LANES]
        k = x_ref[:, key_at + j * LANES : key_at + (j + 1) * LANES]
        qf, kf = q.astype(f32), k.astype(f32)
        q_norm = lax.rsqrt(row_sum(qf * qf) + 1e-06)
        k_norm = lax.rsqrt(row_sum(kf * kf) + 1e-06)
        queries.append((q, q_norm))
        keys.append((k, k_norm))
        packed = jnp.where(col == 2 * value_heads + j, k_norm, packed)
    turned = packed.T
    grams = []
    for j in range(key_heads):
        (q, q_norm), (k, k_norm) = queries[j], keys[j]
        k_row = turned[2 * value_heads + j : 2 * value_heads + j + 1, :]
        kk = contract([(k, k)], 1, 1) * k_norm * k_row
        qk = contract([(q, k)], 1, 1) * (q_norm * LANES ** (-0.5)) * k_row
        grams.append((kk, qk, k_row))
    heads = []
    for i in range(value_heads):
        g = cumulative[:, i : i + 1]
        last = cumulative[BLOCK - 1 : BLOCK, i : i + 1]
        decay = jnp.where(within, jnp.exp(jnp.minimum(g - turned[i : i + 1, :], 0.0)), 0.0)
        beta = strengths[:, value_heads + i : value_heads + i + 1]
        heads.append((decay, beta, jnp.exp(g), jnp.exp(last - g), jnp.exp(last)))
    return row, col, small, strengths, queries, keys, grams, heads


def forward_kernel(
    key_heads, value_heads, x_ref, gain_ref, t_ref, u_ref, h_ref, o_ref, gated_ref, state
):
    group = value_heads // key_heads
    _, _, value_at, gate_at, _ = offsets(key_heads, value_heads)

    @pl.when(pl.program_id(0) == 0)
    def _():
        state[...] = jnp.zeros_like(state)

    row, col, _, _, queries, keys, grams, heads = shared(x_ref, key_heads, value_heads)
    every = range(value_heads)
    strict = row > col
    lower = [
        jnp.where(strict, heads[i][1] * heads[i][0] * grams[i // group][0], 0.0) for i in every
    ]
    eye = (row == col).astype(f32)
    mask = (row >> 1) == (col >> 1)
    inverse = [eye - jnp.where(mask, lower[i], 0.0) for i in every]
    level = 1
    while (1 << level) < BLOCK:
        mask = ((row >> (level + 1)) == (col >> (level + 1))) & ((row >> level) != (col >> level))
        halves = [split(inverse[i]) for i in every]
        middle = [
            contract(full(split(jnp.where(mask, lower[i], 0.0)), halves[i]), 1, 0) for i in every
        ]
        inverse = [
            inverse[i] - contract(full(halves[i], split(middle[i])), 1, 0) for i in every
        ]
        level += 1
    memory = [state[i] for i in every]
    memory_halves = [split(memory[i]) for i in every]
    recalled = [
        contract(left_exact(keys[i // group][0], memory_halves[i]), 1, 0) * keys[i // group][1]
        for i in every
    ]
    asked = [
        contract(left_exact(queries[i // group][0], memory_halves[i]), 1, 0)
        * (queries[i // group][1] * LANES ** (-0.5))
        for i in every
    ]
    target = []
    for i in every:
        _, beta, rising, _, _ = heads[i]
        values = x_ref[:, value_at + i * LANES : value_at + (i + 1) * LANES].astype(f32)
        target.append(beta * (values - rising * recalled[i]))
    update = [contract(full(split(inverse[i]), split(target[i])), 1, 0) for i in every]
    output = [
        heads[i][2] * asked[i]
        + contract(full(split(grams[i // group][1] * heads[i][0]), split(update[i])), 1, 0)
        for i in every
    ]
    for i in every:
        _, _, _, fading, whole = heads[i]
        key, key_norm = keys[i // group]
        t_ref[0, i] = inverse[i]
        u_ref[0, i] = update[i]
        h_ref[0, i] = memory[i]
        o_ref[0, i] = output[i]
        state[i] = whole * memory[i] + contract(
            left_exact(key, split(key_norm * fading * update[i])), 0, 0
        )
        gate = x_ref[:, gate_at + i * LANES : gate_at + (i + 1) * LANES].astype(f32)
        scale = lax.rsqrt(row_sum(output[i] * output[i]) * (1.0 / LANES) + 1e-06)
        gated = output[i] * scale * gain_ref[...] * (gate * sigmoid(gate))
        gated_ref[:, i * LANES : (i + 1) * LANES] = gated.astype(bf16)


def backward_kernel(
    key_heads, value_heads, x_ref, gain_ref, t_ref, u_ref, h_ref, o_ref, grad_ref, y_ref, state
):
    group = value_heads // key_heads
    query_at, key_at, value_at, gate_at, small_at = offsets(key_heads, value_heads)

    @pl.when(pl.program_id(0) == 0)
    def _():
        state[...] = jnp.zeros_like(state)

    row, col, small, strengths, queries, keys, grams, heads = shared(
        x_ref, key_heads, value_heads
    )
    every = range(value_heads)
    strict = row > col
    scale_q = LANES ** (-0.5)
    grad_o = []
    for i in every:
        gate = x_ref[:, gate_at + i * LANES : gate_at + (i + 1) * LANES].astype(f32)
        sigma = sigmoid(gate)
        output = o_ref[0, i]
        inverse_rms = lax.rsqrt(row_sum(output * output) * (1.0 / LANES) + 1e-06)
        normed = output * inverse_rms
        grad = grad_ref[:, i * LANES : (i + 1) * LANES]
        grad_z = grad * normed * gain_ref[...] * (sigma * (1.0 + gate * (1.0 - sigma)))
        y_ref[:, gate_at + i * LANES : gate_at + (i + 1) * LANES] = grad_z.astype(bf16)
        grad_n = grad * gain_ref[...] * (gate * sigma)
        grad_o.append(
            inverse_rms * (grad_n - normed * (row_sum(grad_n * normed) * (1.0 / LANES)))
        )
    grad_h = [state[i] for i in every]
    grad_h2 = [split(grad_h[i]) for i in every]
    grad_o2 = [split(grad_o[i]) for i in every]
    memory = [h_ref[0, i] for i in every]
    memory2 = [split(memory[i]) for i in every]
    update = [u_ref[0, i] for i in every]
    update2 = [split(update[i]) for i in every]
    scores = [grams[i // group][1] * heads[i][0] for i in every]
    key_grad_h = [
        contract(left_exact(keys[i // group][0], grad_h2[i]), 1, 0) * keys[i // group][1]
        for i in every
    ]
    grad_u = [
        contract(full(split(scores[i]), grad_o2[i]), 0, 0) + heads[i][3] * key_grad_h[i]
        for i in every
    ]
    grad_t = [contract(full(split(t_ref[0, i]), split(grad_u[i])), 0, 0) for i in every]
    grad_p = [contract(full(grad_o2[i], update2[i]), 1, 1) for i in every]
    grad_a = [
        jnp.where(strict, -contract(full(split(grad_t[i]), update2[i]), 1, 1), 0.0) for i in every
    ]
    recalled = [
        contract(left_exact(keys[i // group][0], memory2[i]), 1, 0) * keys[i // group][1]
        for i in every
    ]
    asked = [
        contract(left_exact(queries[i // group][0], memory2[i]), 1, 0)
        * (queries[i // group][1] * scale_q)
        for i in every
    ]
    grad_q = [None] * key_heads
    grad_k = [None] * key_heads
    grad_beta = jnp.zeros((BLOCK, LANES), f32)
    grad_g = jnp.zeros((BLOCK, LANES), f32)
    column_sums = jnp.zeros((BLOCK, LANES), f32)

    def add(total, term):
        return term if total is None else total + term

    for i in every:
        j = i // group
        decay, beta, rising, fading, whole = heads[i]
        (q, q_norm), (k, k_norm) = queries[j], keys[j]
        q_scale = q_norm * scale_q
        kk, _, k_row = grams[j]
        values = x_ref[:, value_at + i * LANES : value_at + (i + 1) * LANES].astype(f32)
        grad_w = beta * grad_t[i]
        y_ref[:, value_at + i * LANES : value_at + (i + 1) * LANES] = grad_w.astype(bf16)
        decayed = decay * kk
        beta_term = row_sum(grad_t[i] * (values - rising * recalled[i])) + row_sum(
            grad_a[i] * decayed
        )
        grad_beta = jnp.where(col == value_heads + i, beta_term, grad_beta)
        pulled = grad_p[i] * scores[i] + grad_a[i] * (beta * decayed)
        fade_term = fading * row_sum(update[i] * key_grad_h[i])
        rise_term = rising * (row_sum(grad_o[i] * asked[i]) - row_sum(grad_w * recalled[i]))
        last_term = jnp.sum(fade_term, axis=0, keepdims=True) + whole * jnp.sum(
            row_sum(memory[i] * grad_h[i]), axis=0, keepdims=True
        )
        g_term = row_sum(pulled) + rise_term - fade_term
        g_term = g_term + jnp.where(row[:, :1] == BLOCK - 1, last_term, 0.0)
        grad_g = jnp.where(col == i, g_term, grad_g)
        column_sums = jnp.where(row == i, jnp.sum(pulled, axis=0, keepdims=True), column_sums)
        grad_qk = grad_p[i] * decay
        grad_kk = grad_a[i] * (beta * decay)
        grad_kh = -rising * grad_w
        risen = rising * grad_o[i]
        grad_q[j] = add(
            grad_q[j],
            contract(
                full(split(risen), memory2[i]), 1, 1
            )
            + contract(right_exact(split(grad_qk * k_row), k), 1, 0),
        )
        grad_k[j] = add(
            grad_k[j],
            contract(
                full(split(grad_kh), memory2[i]) + full(split(fading * update[i]), grad_h2[i]), 1, 1
            )
            + contract(right_exact(split(grad_kk * k_row), k), 1, 0)
            + contract(
                right_exact(split(grad_qk * q_scale), q) + right_exact(split(grad_kk * k_norm), k),
                0,
                0,
            ),
        )
        state[i] = whole * grad_h[i] + contract(
            left_exact(k, split(k_norm * grad_kh)) + left_exact(q, split(q_scale * risen)), 0, 0
        )
    for j in range(key_heads):
        (q, q_norm), (k, k_norm) = queries[j], keys[j]
        unit = q.astype(f32) * q_norm
        grad = grad_q[j] * scale_q
        grad = q_norm * (grad - unit * row_sum(unit * grad))
        y_ref[:, query_at + j * LANES : query_at + (j + 1) * LANES] = grad.astype(bf16)
        unit = k.astype(f32) * k_norm
        grad = k_norm * (grad_k[j] - unit * row_sum(unit * grad_k[j]))
        y_ref[:, key_at + j * LANES : key_at + (j + 1) * LANES] = grad.astype(bf16)
    grad_g = grad_g - column_sums.T
    grad_log = jnp.dot(
        (row <= col).astype(f32),
        grad_g,
        precision=lax.Precision.HIGHEST,
        preferred_element_type=f32,
    )
    small_grad = jnp.where(
        col < value_heads, -grad_log * strengths, grad_beta * strengths * (1.0 - strengths)
    )
    y_ref[:, small_at : small_at + LANES] = small_grad.astype(bf16)


def residual_spec(value_heads, place):
    return pl.BlockSpec((1, value_heads, BLOCK, LANES), lambda c: (place(c), 0, 0, 0))


def delta_forward(x, gain, key_heads, value_heads):
    length, columns = x.shape
    blocks = length // BLOCK
    kept = jax.ShapeDtypeStruct((blocks, value_heads, BLOCK, LANES), f32)
    passes = blocks * value_heads * 36
    return pl.pallas_call(
        functools.partial(forward_kernel, key_heads, value_heads),
        grid=(blocks,),
        out_shape=(kept,) * 4 + (jax.ShapeDtypeStruct((length, value_heads * LANES), bf16),),
        in_specs=[
            pl.BlockSpec((BLOCK, columns), lambda c: (c, 0)),
            pl.BlockSpec((1, LANES), lambda c: (0, 0)),
        ],
        out_specs=[residual_spec(value_heads, lambda c: c)] * 4
        + [pl.BlockSpec((BLOCK, value_heads * LANES), lambda c: (c, 0))],
        scratch_shapes=[pltpu.VMEM((value_heads, LANES, LANES), f32)],
        compiler_params=pltpu.CompilerParams(vmem_limit_bytes=40 * 2**20),
        cost_estimate=pl.CostEstimate(
            flops=passes * 8 * LANES**3, bytes_accessed=6 * 2**20, transcendentals=2**20
        ),
    )(x, gain)


def delta_backward(x, gain, kept, grad_gated, key_heads, value_heads):
    length, columns = x.shape
    blocks = length // BLOCK

    def place(c):
        return blocks - 1 - c

    passes = blocks * value_heads * 30
    return pl.pallas_call(
        functools.partial(backward_kernel, key_heads, value_heads),
        grid=(blocks,),
        out_shape=jax.ShapeDtypeStruct((length, columns), bf16),
        in_specs=[
            pl.BlockSpec((BLOCK, columns), lambda c: (place(c), 0)),
            pl.BlockSpec((1, LANES), lambda c: (0, 0)),
        ]
        + [residual_spec(value_heads, place)] * 4
        + [pl.BlockSpec((BLOCK, value_heads * LANES), lambda c: (place(c), 0))],
        out_specs=pl.BlockSpec((BLOCK, columns), lambda c: (place(c), 0)),
        scratch_shapes=[pltpu.VMEM((value_heads, LANES, LANES), f32)],
        compiler_params=pltpu.CompilerParams(vmem_limit_bytes=40 * 2**20),
        cost_estimate=pl.CostEstimate(
            flops=passes * 8 * LANES**3, bytes_accessed=8 * 2**20, transcendentals=2**20
        ),
    )(x, gain, *kept, grad_gated)


def post_norm(hidden, gains):
    inverse_rms = lax.rsqrt(jnp.mean(hidden * hidden, axis=-1, keepdims=True) + 1e-06)
    return hidden * inverse_rms * gains


def expert_backward(rows_in, rows_grad, gate_up, down_proj):
    hidden_units = down_proj.shape[0]
    contract_rows = (((1,), (1,)), ((), ()))
    contract_cols = (((0,), (0,)), ((), ()))
    projected = jnp.dot(rows_in, gate_up, preferred_element_type=jnp.float32)
    gate_part = projected[:, :hidden_units]
    up_part = projected[:, hidden_units:]
    sigma = jax.nn.sigmoid(gate_part)
    activated = gate_part * sigma
    product = (activated * up_part).astype(jnp.bfloat16)
    grad_act = lax.dot_general(
        rows_grad, down_proj, contract_rows, preferred_element_type=jnp.float32
    )
    grad_gate_part = grad_act * up_part * sigma * (1.0 + gate_part * (1.0 - sigma))
    grad_up_part = grad_act * activated
    grad_projected = jnp.concatenate([grad_gate_part, grad_up_part], axis=1).astype(jnp.bfloat16)
    rows_back = lax.dot_general(
        grad_projected, gate_up, contract_rows, preferred_element_type=jnp.float32
    ).astype(jnp.bfloat16)
    weight_gate_up = lax.dot_general(
        rows_in, grad_projected, contract_cols, preferred_element_type=jnp.float32
    ).astype(jnp.bfloat16)
    weight_down = lax.dot_general(
        product, rows_grad, contract_cols, preferred_element_type=jnp.float32
    ).astype(jnp.bfloat16)
    return (rows_back, weight_gate_up, weight_down)

def body(
    hidden_in,
    grad_out,
    post_gain,
    route_ids,
    route_weight,
    gate_up,
    down_proj,
    query_in,
    key_in,
    value_in,
    gate_in,
    decay_logit,
    beta_logit,
    head_gain,
    out_proj,
):
    ctx_count = lax.axis_size("ctx")
    exp_count = lax.axis_size("exp")
    devices = ctx_count * exp_count
    tok_rows = hidden_in.shape[1]
    width = hidden_in.shape[2]
    capacity = max(3, tok_rows // 32)
    key_heads = query_in.shape[2] // LANES // ctx_count
    value_heads = value_in.shape[2] // LANES // ctx_count
    slots = devices * capacity

    def by_device(tensor):
        return tensor[0].reshape(tok_rows, ctx_count, -1)

    packed = [by_device(t) for t in (query_in, key_in, value_in, gate_in, decay_logit, beta_logit)]
    packed.append(jnp.zeros((tok_rows, ctx_count, LANES - 2 * value_heads), bf16))
    outgoing = jnp.concatenate(packed, axis=2).transpose(1, 0, 2)
    columns = outgoing.shape[2]

    flat_hidden = hidden_in[0].astype(f32)
    normed, norm_back = jax.vjp(lambda tensor: post_norm(tensor, post_gain), flat_hidden)
    moe_input = normed.astype(bf16)
    owners = jnp.arange(devices, dtype=jnp.int32)
    named = route_ids[0][:, :, None] == owners[None, None, :]
    picked = jnp.any(named, axis=1)
    weights = jnp.sum(jnp.where(named, route_weight[0][:, :, None], 0.0), axis=1)
    positions = jnp.arange(tok_rows)
    earlier = (positions[:, None] > positions[None, :]).astype(bf16)
    ranks = jnp.dot(earlier, picked.astype(bf16), preferred_element_type=f32)
    places = jnp.arange(capacity, dtype=f32)
    chosen = picked.T[:, None, :] & (ranks.T[:, None, :] == places[None, :, None])
    slot_weight = jnp.sum(jnp.where(chosen, weights.T[:, None, :], 0.0), axis=2).reshape(slots, 1)
    chosen = chosen.reshape(slots, tok_rows).astype(bf16)
    rows_in = jnp.dot(chosen, moe_input, preferred_element_type=f32).astype(bf16)
    rows_grad = (
        jnp.dot(chosen, grad_out[0], preferred_element_type=f32) * slot_weight
    ).astype(bf16)
    sent = jnp.concatenate([rows_in, rows_grad], axis=1).reshape(devices, capacity, 2 * width)
    got = lax.all_to_all(sent, ("ctx", "exp"), split_axis=0, concat_axis=0, tiled=True)
    got = got.reshape(slots, 2 * width)
    x = lax.all_to_all(outgoing, "ctx", split_axis=0, concat_axis=0, tiled=True)
    x = x.reshape(ctx_count * tok_rows, columns)
    gain = head_gain[None, :]
    *kept, gated_round = delta_forward(x, gain, key_heads, value_heads)
    rows_back, grad_gate_up, grad_down = expert_backward(
        got[:, :width], got[:, width:], gate_up[0], down_proj[0]
    )
    returned = lax.all_to_all(
        rows_back.reshape(devices, capacity, width),
        ("ctx", "exp"),
        split_axis=0,
        concat_axis=0,
        tiled=True,
    ).reshape(slots, width)
    moe_grad = lax.dot_general(
        chosen, returned, (((0,), (0,)), ((), ())), preferred_element_type=f32
    )
    (norm_grad,) = norm_back(moe_grad)
    grad_hidden = (grad_out[0].astype(f32) + norm_grad).astype(bf16)[None]
    hidden_all = lax.all_gather(grad_hidden, "ctx", axis=1, tiled=True)[0]
    grad_gated = jnp.dot(hidden_all, out_proj, preferred_element_type=f32)
    y = delta_backward(x, gain, kept, grad_gated, key_heads, value_heads)
    scale_factor = float(tok_rows * devices) ** (-0.5)
    grad_out_proj = lax.psum_scatter(
        (
            scale_factor
            * lax.dot_general(
                hidden_all, gated_round, (((0,), (0,)), ((), ())), preferred_element_type=f32
            )
        ).astype(bf16),
        "exp",
        scatter_dimension=0,
        tiled=True,
    ).astype(f32)
    back = lax.all_to_all(
        y.reshape(ctx_count, tok_rows, columns), "ctx", split_axis=0, concat_axis=0, tiled=True
    )
    parts, start = [], 0
    for count in [key_heads * LANES] * 2 + [value_heads * LANES] * 2 + [value_heads] * 2:
        part = back[:, :, start : start + count].transpose(1, 0, 2)
        parts.append(part.reshape(1, tok_rows, ctx_count * count))
        start += count
    return (grad_hidden, *parts, grad_gate_up[None], grad_down[None], grad_out_proj)


def solution(mesh):
    placed = (
        P("exp", "ctx", None),
        P("exp", "ctx", None),
        P(),
        P("exp", "ctx", None),
        P("exp", "ctx", None),
        P(("ctx", "exp"), None, None),
        P(("ctx", "exp"), None, None),
        P("exp", "ctx", None),
        P("exp", "ctx", None),
        P("exp", "ctx", None),
        P("exp", "ctx", None),
        P("exp", "ctx", None),
        P("exp", "ctx", None),
        P(),
        P(None, "ctx"),
    )
    return jax.shard_map(
        body,
        mesh=mesh,
        in_specs=placed,
        out_specs=(
            P("exp", "ctx", None),
            P("exp", "ctx", None),
            P("exp", "ctx", None),
            P("exp", "ctx", None),
            P("exp", "ctx", None),
            P("exp", "ctx", None),
            P("exp", "ctx", None),
            P(("ctx", "exp"), None, None),
            P(("ctx", "exp"), None, None),
            P("exp", "ctx"),
        ),
        check_vma=False,
    )
```

```python
import functools

import jax
import jax.numpy as jnp
from jax import lax
from jax.experimental import pallas as pl
from jax.experimental.pallas import tpu as pltpu
from jax.sharding import PartitionSpec as P

BLOCK = 128
LANES = 128
f32 = jnp.float32
bf16 = jnp.bfloat16


def split(tensor):
    high = tensor.astype(bf16)
    return high, (tensor - high.astype(f32)).astype(bf16)


def full(left, right):
    return [(left[0], right[0]), (left[1], right[0]), (left[0], right[1])]


def left_exact(left, right):
    return [(left, right[0]), (left, right[1])]


def right_exact(left, right):
    return [(left[0], right), (left[1], right)]


def contract(pairs, left_dim, right_dim):
    left = jnp.concatenate([pair[0] for pair in pairs], axis=left_dim)
    right = jnp.concatenate([pair[1] for pair in pairs], axis=right_dim)
    return lax.dot_general(
        left, right, (((left_dim,), (right_dim,)), ((), ())), preferred_element_type=f32
    )


def sigmoid(tensor):
    return 1.0 / (1.0 + jnp.exp(-tensor))


def row_sum(tensor):
    return jnp.sum(tensor, axis=1, keepdims=True)


def offsets(key_heads, value_heads):
    query_at = 0
    key_at = key_heads * LANES
    value_at = 2 * key_heads * LANES
    gate_at = value_at + value_heads * LANES
    small_at = gate_at + value_heads * LANES
    return query_at, key_at, value_at, gate_at, small_at


def shared(x_ref, key_heads, value_heads):
    query_at, key_at, _, _, small_at = offsets(key_heads, value_heads)
    row = lax.broadcasted_iota(jnp.int32, (BLOCK, BLOCK), 0)
    col = lax.broadcasted_iota(jnp.int32, (BLOCK, BLOCK), 1)
    within = row >= col
    small = x_ref[:, small_at : small_at + LANES].astype(f32)
    log_decay = -(jnp.maximum(small, 0.0) + jnp.log1p(jnp.exp(-jnp.abs(small))))
    log_decay = jnp.where(col < value_heads, log_decay, 0.0)
    cumulative = jnp.dot(
        within.astype(f32),
        log_decay,
        precision=lax.Precision.HIGHEST,
        preferred_element_type=f32,
    )
    strengths = sigmoid(small)
    keys, queries = [], []
    packed = cumulative
    for j in range(key_heads):
        q = x_ref[:, query_at + j * LANES : query_at + (j + 1) * LANES]
        k = x_ref[:, key_at + j * LANES : key_at + (j + 1) * LANES]
        qf, kf = q.astype(f32), k.astype(f32)
        q_norm = lax.rsqrt(row_sum(qf * qf) + 1e-06)
        k_norm = lax.rsqrt(row_sum(kf * kf) + 1e-06)
        queries.append((q, q_norm))
        keys.append((k, k_norm))
        packed = jnp.where(col == 2 * value_heads + j, k_norm, packed)
    turned = packed.T
    grams = []
    for j in range(key_heads):
        (q, q_norm), (k, k_norm) = queries[j], keys[j]
        k_row = turned[2 * value_heads + j : 2 * value_heads + j + 1, :]
        kk = contract([(k, k)], 1, 1) * k_norm * k_row
        qk = contract([(q, k)], 1, 1) * (q_norm * LANES ** (-0.5)) * k_row
        grams.append((kk, qk, k_row))
    heads = []
    for i in range(value_heads):
        g = cumulative[:, i : i + 1]
        last = cumulative[BLOCK - 1 : BLOCK, i : i + 1]
        decay = jnp.where(within, jnp.exp(jnp.minimum(g - turned[i : i + 1, :], 0.0)), 0.0)
        beta = strengths[:, value_heads + i : value_heads + i + 1]
        heads.append((decay, beta, jnp.exp(g), jnp.exp(last - g), jnp.exp(last)))
    return row, col, small, strengths, queries, keys, grams, heads


def forward_kernel(
    key_heads, value_heads, x_ref, gain_ref, t_ref, u_ref, h_ref, o_ref, gated_ref, state
):
    group = value_heads // key_heads
    _, _, value_at, gate_at, _ = offsets(key_heads, value_heads)

    @pl.when(pl.program_id(0) == 0)
    def _():
        state[...] = jnp.zeros_like(state)

    row, col, _, _, queries, keys, grams, heads = shared(x_ref, key_heads, value_heads)
    every = range(value_heads)
    strict = row > col
    lower = [
        jnp.where(strict, heads[i][1] * heads[i][0] * grams[i // group][0], 0.0) for i in every
    ]
    eye = (row == col).astype(f32)
    mask = (row >> 1) == (col >> 1)
    inverse = [eye - jnp.where(mask, lower[i], 0.0) for i in every]
    level = 1
    while (1 << level) < BLOCK:
        mask = ((row >> (level + 1)) == (col >> (level + 1))) & ((row >> level) != (col >> level))
        halves = [split(inverse[i]) for i in every]
        middle = [
            contract(full(split(jnp.where(mask, lower[i], 0.0)), halves[i]), 1, 0) for i in every
        ]
        inverse = [
            inverse[i] - contract(full(halves[i], split(middle[i])), 1, 0) for i in every
        ]
        level += 1
    memory = [state[i] for i in every]
    memory_halves = [split(memory[i]) for i in every]
    recalled = [
        contract(left_exact(keys[i // group][0], memory_halves[i]), 1, 0) * keys[i // group][1]
        for i in every
    ]
    asked = [
        contract(left_exact(queries[i // group][0], memory_halves[i]), 1, 0)
        * (queries[i // group][1] * LANES ** (-0.5))
        for i in every
    ]
    target = []
    for i in every:
        _, beta, rising, _, _ = heads[i]
        values = x_ref[:, value_at + i * LANES : value_at + (i + 1) * LANES].astype(f32)
        target.append(beta * (values - rising * recalled[i]))
    update = [contract(full(split(inverse[i]), split(target[i])), 1, 0) for i in every]
    output = [
        heads[i][2] * asked[i]
        + contract(full(split(grams[i // group][1] * heads[i][0]), split(update[i])), 1, 0)
        for i in every
    ]
    for i in every:
        _, _, _, fading, whole = heads[i]
        key, key_norm = keys[i // group]
        t_ref[0, i] = inverse[i]
        u_ref[0, i] = update[i]
        h_ref[0, i] = memory[i]
        o_ref[0, i] = output[i]
        state[i] = whole * memory[i] + contract(
            left_exact(key, split(key_norm * fading * update[i])), 0, 0
        )
        gate = x_ref[:, gate_at + i * LANES : gate_at + (i + 1) * LANES].astype(f32)
        scale = lax.rsqrt(row_sum(output[i] * output[i]) * (1.0 / LANES) + 1e-06)
        gated = output[i] * scale * gain_ref[...] * (gate * sigmoid(gate))
        gated_ref[:, i * LANES : (i + 1) * LANES] = gated.astype(bf16)


def backward_kernel(
    key_heads, value_heads, x_ref, gain_ref, t_ref, u_ref, h_ref, o_ref, grad_ref, y_ref, state
):
    group = value_heads // key_heads
    query_at, key_at, value_at, gate_at, small_at = offsets(key_heads, value_heads)

    @pl.when(pl.program_id(0) == 0)
    def _():
        state[...] = jnp.zeros_like(state)

    row, col, small, strengths, queries, keys, grams, heads = shared(
        x_ref, key_heads, value_heads
    )
    every = range(value_heads)
    strict = row > col
    scale_q = LANES ** (-0.5)
    grad_o = []
    for i in every:
        gate = x_ref[:, gate_at + i * LANES : gate_at + (i + 1) * LANES].astype(f32)
        sigma = sigmoid(gate)
        output = o_ref[0, i]
        inverse_rms = lax.rsqrt(row_sum(output * output) * (1.0 / LANES) + 1e-06)
        normed = output * inverse_rms
        grad = grad_ref[:, i * LANES : (i + 1) * LANES]
        grad_z = grad * normed * gain_ref[...] * (sigma * (1.0 + gate * (1.0 - sigma)))
        y_ref[:, gate_at + i * LANES : gate_at + (i + 1) * LANES] = grad_z.astype(bf16)
        grad_n = grad * gain_ref[...] * (gate * sigma)
        grad_o.append(
            inverse_rms * (grad_n - normed * (row_sum(grad_n * normed) * (1.0 / LANES)))
        )
    grad_h = [state[i] for i in every]
    grad_h2 = [split(grad_h[i]) for i in every]
    grad_o2 = [split(grad_o[i]) for i in every]
    memory = [h_ref[0, i] for i in every]
    memory2 = [split(memory[i]) for i in every]
    update = [u_ref[0, i] for i in every]
    update2 = [split(update[i]) for i in every]
    scores = [grams[i // group][1] * heads[i][0] for i in every]
    key_grad_h = [
        contract(left_exact(keys[i // group][0], grad_h2[i]), 1, 0) * keys[i // group][1]
        for i in every
    ]
    grad_u = [
        contract(full(split(scores[i]), grad_o2[i]), 0, 0) + heads[i][3] * key_grad_h[i]
        for i in every
    ]
    grad_t = [contract(full(split(t_ref[0, i]), split(grad_u[i])), 0, 0) for i in every]
    grad_p = [contract(full(grad_o2[i], update2[i]), 1, 1) for i in every]
    grad_a = [
        jnp.where(strict, -contract(full(split(grad_t[i]), update2[i]), 1, 1), 0.0) for i in every
    ]
    recalled = [
        contract(left_exact(keys[i // group][0], memory2[i]), 1, 0) * keys[i // group][1]
        for i in every
    ]
    asked = [
        contract(left_exact(queries[i // group][0], memory2[i]), 1, 0)
        * (queries[i // group][1] * scale_q)
        for i in every
    ]
    grad_q = [None] * key_heads
    grad_k = [None] * key_heads
    grad_beta = jnp.zeros((BLOCK, LANES), f32)
    grad_g = jnp.zeros((BLOCK, LANES), f32)
    column_sums = jnp.zeros((BLOCK, LANES), f32)

    def add(total, term):
        return term if total is None else total + term

    for i in every:
        j = i // group
        decay, beta, rising, fading, whole = heads[i]
        (q, q_norm), (k, k_norm) = queries[j], keys[j]
        q_scale = q_norm * scale_q
        kk, _, k_row = grams[j]
        values = x_ref[:, value_at + i * LANES : value_at + (i + 1) * LANES].astype(f32)
        grad_w = beta * grad_t[i]
        y_ref[:, value_at + i * LANES : value_at + (i + 1) * LANES] = grad_w.astype(bf16)
        decayed = decay * kk
        beta_term = row_sum(grad_t[i] * (values - rising * recalled[i])) + row_sum(
            grad_a[i] * decayed
        )
        grad_beta = jnp.where(col == value_heads + i, beta_term, grad_beta)
        pulled = grad_p[i] * scores[i] + grad_a[i] * (beta * decayed)
        fade_term = fading * row_sum(update[i] * key_grad_h[i])
        rise_term = rising * (row_sum(grad_o[i] * asked[i]) - row_sum(grad_w * recalled[i]))
        last_term = jnp.sum(fade_term, axis=0, keepdims=True) + whole * jnp.sum(
            row_sum(memory[i] * grad_h[i]), axis=0, keepdims=True
        )
        g_term = row_sum(pulled) + rise_term - fade_term
        g_term = g_term + jnp.where(row[:, :1] == BLOCK - 1, last_term, 0.0)
        grad_g = jnp.where(col == i, g_term, grad_g)
        column_sums = jnp.where(row == i, jnp.sum(pulled, axis=0, keepdims=True), column_sums)
        grad_qk = grad_p[i] * decay
        grad_kk = grad_a[i] * (beta * decay)
        grad_kh = -rising * grad_w
        risen = rising * grad_o[i]
        grad_q[j] = add(
            grad_q[j],
            contract(
                full(split(risen), memory2[i]), 1, 1
            )
            + contract(right_exact(split(grad_qk * k_row), k), 1, 0),
        )
        grad_k[j] = add(
            grad_k[j],
            contract(
                full(split(grad_kh), memory2[i]) + full(split(fading * update[i]), grad_h2[i]), 1, 1
            )
            + contract(right_exact(split(grad_kk * k_row), k), 1, 0)
            + contract(
                right_exact(split(grad_qk * q_scale), q) + right_exact(split(grad_kk * k_norm), k),
                0,
                0,
            ),
        )
        state[i] = whole * grad_h[i] + contract(
            left_exact(k, split(k_norm * grad_kh)) + left_exact(q, split(q_scale * risen)), 0, 0
        )
    for j in range(key_heads):
        (q, q_norm), (k, k_norm) = queries[j], keys[j]
        unit = q.astype(f32) * q_norm
        grad = grad_q[j] * scale_q
        grad = q_norm * (grad - unit * row_sum(unit * grad))
        y_ref[:, query_at + j * LANES : query_at + (j + 1) * LANES] = grad.astype(bf16)
        unit = k.astype(f32) * k_norm
        grad = k_norm * (grad_k[j] - unit * row_sum(unit * grad_k[j]))
        y_ref[:, key_at + j * LANES : key_at + (j + 1) * LANES] = grad.astype(bf16)
    grad_g = grad_g - column_sums.T
    grad_log = jnp.dot(
        (row <= col).astype(f32),
        grad_g,
        precision=lax.Precision.HIGHEST,
        preferred_element_type=f32,
    )
    small_grad = jnp.where(
        col < value_heads, -grad_log * strengths, grad_beta * strengths * (1.0 - strengths)
    )
    y_ref[:, small_at : small_at + LANES] = small_grad.astype(bf16)


def residual_spec(value_heads, place):
    return pl.BlockSpec((1, value_heads, BLOCK, LANES), lambda c: (place(c), 0, 0, 0))


def delta_forward(x, gain, key_heads, value_heads):
    length, columns = x.shape
    blocks = length // BLOCK
    kept = jax.ShapeDtypeStruct((blocks, value_heads, BLOCK, LANES), f32)
    passes = blocks * value_heads * 36
    return pl.pallas_call(
        functools.partial(forward_kernel, key_heads, value_heads),
        grid=(blocks,),
        out_shape=(kept,) * 4 + (jax.ShapeDtypeStruct((length, value_heads * LANES), bf16),),
        in_specs=[
            pl.BlockSpec((BLOCK, columns), lambda c: (c, 0)),
            pl.BlockSpec((1, LANES), lambda c: (0, 0)),
        ],
        out_specs=[residual_spec(value_heads, lambda c: c)] * 4
        + [pl.BlockSpec((BLOCK, value_heads * LANES), lambda c: (c, 0))],
        scratch_shapes=[pltpu.VMEM((value_heads, LANES, LANES), f32)],
        compiler_params=pltpu.CompilerParams(vmem_limit_bytes=40 * 2**20),
        cost_estimate=pl.CostEstimate(
            flops=passes * 8 * LANES**3, bytes_accessed=6 * 2**20, transcendentals=2**20
        ),
    )(x, gain)


def delta_backward(x, gain, kept, grad_gated, key_heads, value_heads):
    length, columns = x.shape
    blocks = length // BLOCK

    def place(c):
        return blocks - 1 - c

    passes = blocks * value_heads * 30
    return pl.pallas_call(
        functools.partial(backward_kernel, key_heads, value_heads),
        grid=(blocks,),
        out_shape=jax.ShapeDtypeStruct((length, columns), bf16),
        in_specs=[
            pl.BlockSpec((BLOCK, columns), lambda c: (place(c), 0)),
            pl.BlockSpec((1, LANES), lambda c: (0, 0)),
        ]
        + [residual_spec(value_heads, place)] * 4
        + [pl.BlockSpec((BLOCK, value_heads * LANES), lambda c: (place(c), 0))],
        out_specs=pl.BlockSpec((BLOCK, columns), lambda c: (place(c), 0)),
        scratch_shapes=[pltpu.VMEM((value_heads, LANES, LANES), f32)],
        compiler_params=pltpu.CompilerParams(vmem_limit_bytes=40 * 2**20),
        cost_estimate=pl.CostEstimate(
            flops=passes * 8 * LANES**3, bytes_accessed=8 * 2**20, transcendentals=2**20
        ),
    )(x, gain, *kept, grad_gated)


def post_norm(hidden, gains):
    inverse_rms = lax.rsqrt(jnp.mean(hidden * hidden, axis=-1, keepdims=True) + 1e-06)
    return hidden * inverse_rms * gains


def expert_backward(rows_in, rows_grad, gate_up, down_proj):
    hidden_units = down_proj.shape[0]
    contract_rows = (((1,), (1,)), ((), ()))
    contract_cols = (((0,), (0,)), ((), ()))
    projected = jnp.dot(rows_in, gate_up, preferred_element_type=jnp.float32)
    gate_part = projected[:, :hidden_units]
    up_part = projected[:, hidden_units:]
    sigma = jax.nn.sigmoid(gate_part)
    activated = gate_part * sigma
    product = (activated * up_part).astype(jnp.bfloat16)
    grad_act = lax.dot_general(
        rows_grad, down_proj, contract_rows, preferred_element_type=jnp.float32
    )
    grad_gate_part = grad_act * up_part * sigma * (1.0 + gate_part * (1.0 - sigma))
    grad_up_part = grad_act * activated
    grad_projected = jnp.concatenate([grad_gate_part, grad_up_part], axis=1).astype(jnp.bfloat16)
    rows_back = lax.dot_general(
        grad_projected, gate_up, contract_rows, preferred_element_type=jnp.float32
    ).astype(jnp.bfloat16)
    weight_gate_up = lax.dot_general(
        rows_in, grad_projected, contract_cols, preferred_element_type=jnp.float32
    ).astype(jnp.bfloat16)
    weight_down = lax.dot_general(
        product, rows_grad, contract_cols, preferred_element_type=jnp.float32
    ).astype(jnp.bfloat16)
    return (rows_back, weight_gate_up, weight_down)

def body(
    hidden_in,
    grad_out,
    post_gain,
    route_ids,
    route_weight,
    gate_up,
    down_proj,
    query_in,
    key_in,
    value_in,
    gate_in,
    decay_logit,
    beta_logit,
    head_gain,
    out_proj,
):
    ctx_count = lax.axis_size("ctx")
    exp_count = lax.axis_size("exp")
    devices = ctx_count * exp_count
    tok_rows = hidden_in.shape[1]
    width = hidden_in.shape[2]
    capacity = max(3, tok_rows // 32)
    key_heads = query_in.shape[2] // LANES // ctx_count
    value_heads = value_in.shape[2] // LANES // ctx_count
    slots = devices * capacity

    received = [
        lax.all_to_all(t, "ctx", split_axis=2, concat_axis=1, tiled=True)[0]
        for t in (query_in, key_in, value_in, gate_in, decay_logit, beta_logit)
    ]
    received.append(jnp.zeros((ctx_count * tok_rows, LANES - 2 * value_heads), bf16))
    x = jnp.concatenate(received, axis=1)
    columns = x.shape[1]

    flat_hidden = hidden_in[0].astype(f32)
    normed, norm_back = jax.vjp(lambda tensor: post_norm(tensor, post_gain), flat_hidden)
    moe_input = normed.astype(bf16)
    owners = jnp.arange(devices, dtype=jnp.int32)
    named = route_ids[0][:, :, None] == owners[None, None, :]
    picked = jnp.any(named, axis=1)
    weights = jnp.sum(jnp.where(named, route_weight[0][:, :, None], 0.0), axis=1)
    positions = jnp.arange(tok_rows)
    earlier = (positions[:, None] > positions[None, :]).astype(bf16)
    ranks = jnp.dot(earlier, picked.astype(bf16), preferred_element_type=f32)
    places = jnp.arange(capacity, dtype=f32)
    chosen = picked.T[:, None, :] & (ranks.T[:, None, :] == places[None, :, None])
    slot_weight = jnp.sum(jnp.where(chosen, weights.T[:, None, :], 0.0), axis=2).reshape(slots, 1)
    chosen = chosen.reshape(slots, tok_rows).astype(bf16)
    rows_in = jnp.dot(chosen, moe_input, preferred_element_type=f32).astype(bf16)
    rows_grad = (
        jnp.dot(chosen, grad_out[0], preferred_element_type=f32) * slot_weight
    ).astype(bf16)
    sent = jnp.concatenate([rows_in, rows_grad], axis=1).reshape(devices, capacity, 2 * width)
    got = lax.all_to_all(sent, ("ctx", "exp"), split_axis=0, concat_axis=0, tiled=True)
    got = got.reshape(slots, 2 * width)
    gain = head_gain[None, :]
    *kept, gated_round = delta_forward(x, gain, key_heads, value_heads)
    rows_back, grad_gate_up, grad_down = expert_backward(
        got[:, :width], got[:, width:], gate_up[0], down_proj[0]
    )
    returned = lax.all_to_all(
        rows_back.reshape(devices, capacity, width),
        ("ctx", "exp"),
        split_axis=0,
        concat_axis=0,
        tiled=True,
    ).reshape(slots, width)
    moe_grad = lax.dot_general(
        chosen, returned, (((0,), (0,)), ((), ())), preferred_element_type=f32
    )
    (norm_grad,) = norm_back(moe_grad)
    grad_hidden = (grad_out[0].astype(f32) + norm_grad).astype(bf16)[None]
    hidden_all = lax.all_gather(grad_hidden, "ctx", axis=1, tiled=True)[0]
    grad_gated = jnp.dot(hidden_all, out_proj, preferred_element_type=f32)
    y = delta_backward(x, gain, kept, grad_gated, key_heads, value_heads)
    scale_factor = float(tok_rows * devices) ** (-0.5)
    grad_out_proj = lax.psum_scatter(
        (
            scale_factor
            * lax.dot_general(
                hidden_all, gated_round, (((0,), (0,)), ((), ())), preferred_element_type=f32
            )
        ).astype(bf16),
        "exp",
        scatter_dimension=0,
        tiled=True,
    ).astype(f32)
    back = lax.all_to_all(
        y.reshape(ctx_count, tok_rows, columns), "ctx", split_axis=0, concat_axis=0, tiled=True
    )
    parts, start = [], 0
    for count in [key_heads * LANES] * 2 + [value_heads * LANES] * 2 + [value_heads] * 2:
        part = back[:, :, start : start + count].transpose(1, 0, 2)
        parts.append(part.reshape(1, tok_rows, ctx_count * count))
        start += count
    return (grad_hidden, *parts, grad_gate_up[None], grad_down[None], grad_out_proj)


def solution(mesh):
    placed = (
        P("exp", "ctx", None),
        P("exp", "ctx", None),
        P(),
        P("exp", "ctx", None),
        P("exp", "ctx", None),
        P(("ctx", "exp"), None, None),
        P(("ctx", "exp"), None, None),
        P("exp", "ctx", None),
        P("exp", "ctx", None),
        P("exp", "ctx", None),
        P("exp", "ctx", None),
        P("exp", "ctx", None),
        P("exp", "ctx", None),
        P(),
        P(None, "ctx"),
    )
    return jax.shard_map(
        body,
        mesh=mesh,
        in_specs=placed,
        out_specs=(
            P("exp", "ctx", None),
            P("exp", "ctx", None),
            P("exp", "ctx", None),
            P("exp", "ctx", None),
            P("exp", "ctx", None),
            P("exp", "ctx", None),
            P("exp", "ctx", None),
            P(("ctx", "exp"), None, None),
            P(("ctx", "exp"), None, None),
            P("exp", "ctx"),
        ),
        check_vma=False,
    )
```
